256 devices in a mesh: section: 4 (over z_lo, core), mp: 64 (over y, z_hi, x).
Axes of the slice: x: 4, y: 4, z: 8 (z_hi: 4, z_lo: 2; z = z_hi * 2 + z_lo), core: 2. Of those that a mesh axis runs over, the one named last changes fastest.
Arguments:
- query_rows: bfloat16 [32768, 3200], P(('mp', 'section')), may hold values from -4.5 to 4.5
- key_rows: bfloat16 [32768, 3200], P(('mp', 'section')), may hold values from -4.5 to 4.5
- value_rows: bfloat16 [32768, 3200], P(('mp', 'section')), may hold values from -6 to 6
- image_lengths: int32 [32, 3], replicated, may hold values from 1 to 512, 1024 in all within a row
- dest_group: int32 [32768, 1], P(('mp', 'section')), may hold values from 0 to 3; in each aligned block of 128 rows (0 to 127, 128 to 255, ...) at most 64 rows name the same one
- proj_weight: bfloat16 [3200, 8192], P('mp', 'section'), may hold values from -0.109375 to 0.109375
- llm_grad: bfloat16 [4, 16384, 8192], P('section', 'mp'), may hold values from -6 to 6
Outputs:
- visual_embeds: bfloat16 [4, 16384, 8192], P('section', 'mp')
- visual_grad: bfloat16 [32768, 3200], P(('mp', 'section'))
The draws below stay inside these ranges and needn't reach their ends.
Inputs may be any that keep to these rules, and one draw needn't show every extreme that they name: `image_lengths`: the entries of each block sum to 1024; each block has one image of exactly half of 1024 patches. `dest_group`: among the rows of one device (128 consecutive rows) no group is named by more than 64 rows, and in every draw some group is named by exactly 64 rows of some device.
All inputs are finite; a program needn't handle non-finite values.
Results may differ from the reference program's by a relative error of at most 0.0057.
Values may be sent and summed in bfloat16 or wider, within the bound.
A program may use at most 128 MiB of HBM per device.

```python
import math
import jax
import jax.numpy as jnp
import numpy as np
from jax import lax

DV = 3200
HEADS = 25
HEAD_DIM = 128
DL = 8192
BLOCK = 1024
ROWS_DEV = 128
IMGS = 3
CAP = 64
TILES = 256
BLOCKS = 32
N_SECTION = 4
N_MP = 64


def draw_query_rows(key, part):
    key = jax.random.fold_in(key, 11)
    base = jnp.clip(jax.random.normal(key, (TILES * ROWS_DEV, DV), jnp.float32), -4.5, 4.5)
    return base.astype(jnp.bfloat16)


def draw_key_rows(key, part):
    key = jax.random.fold_in(key, 23)
    base = jnp.clip(jax.random.normal(key, (TILES * ROWS_DEV, DV), jnp.float32), -4.5, 4.5)
    return base.astype(jnp.bfloat16)


def block_levels(rng, shape, shards, least, top_value):
    loudness = 1.0
    for position, blocks in shards:
        draws = jax.random.uniform(jax.random.fold_in(jax.random.fold_in(rng, 6), position), (blocks,), jnp.float32, least / len(shards), top_value / len(shards))
        loudness = loudness * jnp.repeat(jnp.exp(draws), shape[position] // blocks).reshape((-1,) + (1,) * (len(shape) - 1 - position))
    return loudness


def length_profile(number_of, total, bound, lean):
    portions = [(1 << 20) // math.isqrt(standing ** lean) + 1 for standing in range(2, number_of + 1)]
    spare, holding = total - bound - (number_of - 1), [1] * (number_of - 1)
    while spare > 0:
        free = [i for i in range(number_of - 1) if holding[i] < bound]
        pool, left = sum([portions[i] for i in free]), spare
        for i in free:
            extra = min(bound - holding[i], max(1, left * portions[i] // pool), spare)
            holding[i] = holding[i] + extra
            spare = spare - extra
    return np.array([bound] + holding)


def ragged_sizes(key, count, total, reach, slope):
    if count == 2:
        one = jax.random.randint(key, (), max(1, total - reach), min(reach, total - 1) + 1)
        return jnp.stack([one, total - one])
    lengths = jnp.asarray(length_profile(count, total, reach, slope), jnp.int32)
    twos = (count - 1) // 2
    donor, receiver = lengths[1:1 + 2 * twos:2], lengths[2:2 + 2 * twos:2]
    room = jnp.minimum(donor - 1, reach - receiver)
    moved = jax.random.randint(jax.random.fold_in(key, 1), (twos,), 0, 1 << 20) % (room + 1)
    lengths = lengths.at[1:1 + 2 * twos:2].set(donor - moved).at[2:2 + 2 * twos:2].set(receiver + moved)
    return lengths[jax.random.permutation(jax.random.fold_in(key, 2), count)]


def shared_out(key, own, number, rows, number_of, top, reach, lean):
    sequence = jax.random.permutation(key, number_of)
    crowded, ordinary = shares(number_of, rows * top, reach, lean, True), shares(number_of, rows * top, reach, lean, False)
    places = jnp.arange(number_of)

    def named(tallies, turn):
        used = int((tallies > 0).sum())
        fixed = max(1, used // 4)
        shifted = fixed + (places - fixed + turn * (used - fixed)) % max(1, number_of - fixed)
        return jnp.zeros((number_of,), jnp.int32).at[sequence[jnp.where(places < fixed, places, shifted)]].set(jnp.asarray(tallies, jnp.int32))

    tallies = jnp.where(number % 4 == 0, named(crowded, number // 4), named(ordinary, number - number // 4 - 1))
    mixed = jax.random.permutation(jax.random.fold_in(own, 3), number_of)
    giver, taker = mixed[0:number_of // 2 * 2:2], mixed[1:number_of // 2 * 2:2]
    slack = jnp.minimum(tallies[giver] - 1, reach - tallies[taker]) // 2
    slack = jnp.where((giver == sequence[0]) | (taker == sequence[0]) | (tallies[taker] == 0), 0, jnp.maximum(slack, 0))
    shifted = jax.random.randint(jax.random.fold_in(own, 4), (number_of // 2,), 0, 1 << 20) % (slack + 1)
    tallies = tallies.at[giver].add(-shifted).at[taker].add(shifted)
    items = jnp.searchsorted(jnp.cumsum(tallies), jnp.arange(rows * top), side="right").astype(jnp.int32)
    listing = items.reshape(top, rows).T
    listing = listing[jax.random.permutation(jax.random.fold_in(own, 1), rows)]
    turn = jax.random.randint(jax.random.fold_in(own, 2), (rows, 1), 0, top)
    return jnp.take_along_axis(listing, (jnp.arange(top)[None, :] + turn) % top, axis=1)


def shares(number_of, total, reach, lean, full):
    loads = [(1 << 20) // math.isqrt(standing ** lean) + 1 for standing in range(1, number_of + 1)]
    largest = reach if full else min(reach, max(-(-total // number_of), total * loads[0] // sum(loads)))
    least = 1 if total - largest >= number_of - 1 else 0
    counts, spare = [largest] + [least] * (number_of - 1), total - largest - least * (number_of - 1)
    while spare > 0:
        candidates = [i for i in range(1, number_of) if counts[i] < largest] or [i for i in range(1, number_of) if counts[i] < reach]
        whole, remaining = sum([loads[i] for i in candidates]), spare
        for i in candidates:
            addition = min(reach - counts[i], max(1, remaining * loads[i] // whole), spare)
            counts[i] = counts[i] + addition
            spare = spare - addition
    return np.array(counts)


def gaussian(own_key, extent, scale, limit, split=(), held_as=jnp.bfloat16):
    entries = scale * jax.random.normal(own_key, extent, jnp.float32)
    if split:
        entries = entries * block_levels(own_key, extent, split, -0.22, 0.18)
    return jnp.clip(entries, -limit, limit).astype(held_as)


def setup_inputs(seed: int = 0) -> dict:
    splits = jax.random.split(jax.random.key(seed), 8)
    query_rows = draw_query_rows(jax.random.fold_in(splits[7], 71), 0)
    key_rows = draw_key_rows(jax.random.fold_in(splits[7], 71), 0)
    value_rows = gaussian(splits[2], (TILES * ROWS_DEV, DV), 1.0, 6.0, ((0, 256),))
    image_lengths = jax.vmap(lambda own: ragged_sizes(own, IMGS, BLOCK, BLOCK // 2, 2))(jax.random.split(splits[3], BLOCKS)).reshape((BLOCKS, IMGS)).astype(jnp.int32)
    dest_group_keys = jax.random.split(jax.random.fold_in(splits[4], 1), (TILES * ROWS_DEV) // ROWS_DEV)
    dest_group_turns = jax.random.permutation(jax.random.fold_in(splits[4], 3), (TILES * ROWS_DEV) // ROWS_DEV)
    dest_group = jax.vmap(lambda own, number: shared_out(jax.random.fold_in(splits[4], 2), own, number, ROWS_DEV, N_SECTION, 1, CAP, 2))(dest_group_keys, dest_group_turns).reshape((TILES * ROWS_DEV, 1))
    proj_weight = gaussian(splits[5], (DV, DL), DV ** -0.5, 0.109375, ((0, 64), (1, 4)))
    llm_grad = gaussian(splits[6], (N_SECTION, TILES * CAP, DL), 1.0, 6.0, ((0, 4), (1, 64)))
    return {"query_rows": query_rows, "key_rows": key_rows, "value_rows": value_rows, "image_lengths": image_lengths, "dest_group": dest_group, "proj_weight": proj_weight, "llm_grad": llm_grad}


def image_index(img_lengths, rows_count):
    positions = jnp.arange(rows_count, dtype=jnp.int32)
    ends = jnp.cumsum(img_lengths).astype(jnp.int32)
    return jnp.sum((positions[:, None] >= ends[None, :]).astype(jnp.int32), axis=1)


def head_attention(query_head, key_head, value_head, same_image):
    scores = jnp.dot(query_head, key_head.T, preferred_element_type=jnp.float32) * (HEAD_DIM ** -0.5)
    scores = jnp.where(same_image, scores, -1e30)
    row_max = jnp.max(scores, axis=1, keepdims=True)
    raised = jnp.exp(scores - row_max)
    totals = jnp.sum(raised, axis=1, keepdims=True)
    weights_bf = (raised / totals).astype(jnp.bfloat16)
    return jnp.dot(weights_bf, value_head, preferred_element_type=jnp.float32).astype(jnp.bfloat16)


def attend_block(inputs):
    query_part, key_part, value_part, img_lengths = inputs
    rows_count = query_part.shape[0]
    segment = image_index(img_lengths, rows_count)
    same_image = segment[:, None] == segment[None, :]
    heads = jnp.stack([query_part, key_part, value_part]).reshape(3, rows_count, HEADS, HEAD_DIM).transpose(2, 0, 1, 3)

    def one_head(triple):
        return head_attention(triple[0], triple[1], triple[2], same_image)

    mixed = lax.map(one_head, heads)
    return mixed.transpose(1, 0, 2).reshape(rows_count, HEADS * HEAD_DIM)


def slot_matrix(dest_col, groups, capacity):
    dest_ids = dest_col[:, 0]
    onehot = (dest_ids[:, None] == jnp.arange(groups, dtype=jnp.int32)[None, :]).astype(jnp.int32)
    earlier = jnp.cumsum(onehot, axis=0) - onehot
    slot_ids = jnp.sum(earlier * onehot, axis=1)
    target = dest_ids * capacity + slot_ids
    slots = jnp.arange(groups * capacity, dtype=jnp.int32)
    return (slots[:, None] == target[None, :]).astype(jnp.bfloat16)


def reference(query_rows, key_rows, value_rows, image_lengths, dest_group, proj_weight, llm_grad):
    tiles = N_SECTION * N_MP
    blocks = tiles * ROWS_DEV // BLOCK
    mixing = lax.map(attend_block, (query_rows.reshape(blocks, BLOCK, DV), key_rows.reshape(blocks, BLOCK, DV), value_rows.reshape(blocks, BLOCK, DV), image_lengths))
    mixing_tiles = mixing.reshape(tiles, ROWS_DEV, DV)
    dest_tiles = dest_group.reshape(tiles, ROWS_DEV, 1)
    grad_tiles = llm_grad.reshape(N_SECTION, tiles, CAP, DL).transpose(1, 0, 2, 3).reshape(tiles, N_SECTION * CAP, DL)

    def per_tile(inputs):
        mixing_part, dest_col, grad_part = inputs
        projected = jnp.dot(mixing_part, proj_weight, preferred_element_type=jnp.float32).astype(jnp.bfloat16)
        placing = slot_matrix(dest_col, N_SECTION, CAP)
        sent = jnp.dot(placing, projected, preferred_element_type=jnp.float32).astype(jnp.bfloat16)
        row_grad = lax.dot_general(placing, grad_part, (((0,), (0,)), ((), ())), preferred_element_type=jnp.float32).astype(jnp.bfloat16)
        back = lax.dot_general(row_grad, proj_weight, (((1,), (1,)), ((), ())), preferred_element_type=jnp.float32)
        return sent, back.astype(jnp.bfloat16)

    sent, grads = lax.map(per_tile, (mixing_tiles, dest_tiles, grad_tiles))
    embeds = sent.reshape(tiles, N_SECTION, CAP, DL).transpose(1, 0, 2, 3).reshape(N_SECTION, tiles * CAP, DL)
    return embeds, grads.reshape(tiles * ROWS_DEV, DV)
```

```python
import functools

import jax
import jax.numpy as jnp
from jax import lax
from jax.experimental import pallas as pl
from jax.experimental.pallas import tpu as pltpu
from jax.sharding import PartitionSpec as P

MESH = pl.DeviceIdType.MESH
BF = jnp.bfloat16
F32 = jnp.float32
HD = 128
BLOCK = 1024
TILE = 128
CAP = 64
DV = 3200
OWN = 384
LAST = 3072
ROWS = 400
COLS = 256
SIZES = {"x": 4, "y": 4, "z": 8}
PARTS = (
    (0, 48, "xyz", 0),
    (48, 48, "xyz", 0),
    (96, 32, "zxy", 1),
    (128, 64, "zyx", 0),
    (192, 64, "zyx", 0),
    (256, 80, "zxy", 0),
    (336, 64, "zxy", 1),
)
K_PARTS = ((0, 128, 0), (128, 128, 1024), (256, 128, 2048), (384, 16, 3072))


def place():
    section, mp = lax.axis_index("section"), lax.axis_index("mp")
    return {
        "x": mp % 4,
        "y": mp // 16,
        "z": ((mp // 4) % 4) * 2 + section // 2,
        "c": section % 2,
    }


def device(at):
    return {
        "mp": (at["y"] * 4 + at["z"] // 2) * 4 + at["x"],
        "section": (at["z"] % 2) * 2 + at["c"],
    }


def one_hot(condition):
    return jnp.where(condition, 1.0, 0.0).astype(BF)


def dot(a, b):
    return jnp.dot(a, b, preferred_element_type=F32)


def dot_nt(a, b):
    return lax.dot_general(a, b, (((1,), (1,)), ((), ())), preferred_element_type=F32)


def placing(dest):
    group = lax.broadcasted_iota(jnp.int32, (8, TILE), 0)
    named = jnp.where(group == dest, 1.0, 0.0)
    before = one_hot(
        lax.broadcasted_iota(jnp.int32, (TILE, TILE), 0)
        < lax.broadcasted_iota(jnp.int32, (TILE, TILE), 1)
    )
    earlier = dot(named.astype(BF), before)
    rank = jnp.sum(named * earlier, axis=0, keepdims=True)
    target = dest[0:1].astype(F32) * float(CAP) + rank
    slots = lax.broadcasted_iota(jnp.int32, (4 * CAP, TILE), 0).astype(F32)
    return jnp.where(slots == target, 1.0, 0.0)


def segments(shape, axis, start, ends):
    rows = lax.broadcasted_iota(jnp.int32, shape, axis) + start
    count = jnp.zeros(shape, jnp.int32)
    for end in ends:
        count = count + jnp.where(rows >= end, 1, 0)
    return count


def attend(q, k, v, same):
    scores = dot_nt(q, k) * HD ** (-0.5)
    scores = jnp.where(same, scores, -1e30)
    raised = jnp.exp(scores - jnp.max(scores, axis=1, keepdims=True))
    inverse = 1.0 / jnp.sum(raised, axis=1, keepdims=True)
    return dot((raised * inverse).astype(BF), v).astype(BF)


class Copies:
    def __init__(self, send, recv):
        self.send, self.recv, self.count, self.sent = send, recv, 0, []

    def new(self):
        self.count += 1
        return self.count - 1

    def make(self, index, src, dst, to):
        return pltpu.make_async_remote_copy(
            src_ref=src,
            dst_ref=dst,
            send_sem=self.send.at[index],
            recv_sem=self.recv.at[index],
            device_id=to,
            device_id_type=MESH,
        )

    def start(self, index, src, dst, to):
        copy = self.make(index, src, dst, to)
        copy.start()
        self.sent.append(copy)
        return copy

    def arrive(self, index, dst, to):
        self.make(index, dst, dst, to).wait_recv()

    def drain(self):
        for copy in self.sent:
            copy.wait_send()
        self.sent = []


def ring(copies, buf, me, part):
    first, rows, order, flip = part
    done = []
    for axis in order:
        size = SIZES[axis]
        even = 1 - 2 * (me[axis] % 2)
        step = -even if flip else even
        near = {**me, axis: (me[axis] + step + size) % size}
        far = {**me, axis: (me[axis] - step + size) % size}

        def block(offset):
            at = {
                **{a: me[a] for a in SIZES},
                axis: (me[axis] + offset * step + size) % size,
            }
            index = []
            for a in ("y", "z", "x"):
                if a in done:
                    index += [slice(None)] * (2 if a == "z" else 1)
                elif a == "z":
                    index += [at[a] // 4, at[a] % 4]
                else:
                    index += [at[a]]
            return buf.at[(*index, pl.ds(first, rows), slice(None))]

        to_far = [copies.new() for _ in range(size // 2)]
        to_near = [copies.new() for _ in range(size // 2 - 1)]
        copies.start(to_far[0], block(0), block(0), device(far))
        copies.start(to_near[0], block(0), block(0), device(near))
        for k in range(size // 2):
            yield
            if k < size // 2 - 1:
                copies.arrive(to_near[k], block(k + 1), device(near))
                copies.start(to_far[k + 1], block(k + 1), block(k + 1), device(far))
            copies.arrive(to_far[k], block(-(k + 1)), device(far))
            if k + 1 < size // 2 - 1:
                copies.start(
                    to_near[k + 1], block(-(k + 1)), block(-(k + 1)), device(near)
                )
        done = done + [axis]


def kernel(
    lengths,
    dest_ref,
    q_ref,
    k_ref,
    v_ref,
    w_ref,
    grad_ref,
    embeds_ref,
    vgrad_ref,
    weight,
    w_pieces,
    qkv,
    kv_last,
    q_last,
    dests,
    mixed,
    staged,
    staged_last,
    slots,
    lhs,
    grads,
    embeds,
    back,
    back_in,
    returned,
    send_sem,
    recv_sem,
    local_sem,
):
    me = place()
    section, mp = lax.axis_index("section"), lax.axis_index("mp")
    core = me["c"]
    local = (mp % 2) * 4 + section
    member = mp % 8
    copies = Copies(send_sem, recv_sem)
    sibling = device({**me, "c": 1 - core})

    def in_block(index):
        return {"mp": mp - mp % 2 + index // 4, "section": index % 4}

    def in_octet(index):
        return {"mp": mp - mp % 8 + index, "section": section}

    def in_section(index):
        return {"mp": mp, "section": index}

    greeted = [in_block((local + k) % 8) for k in range(1, 8)]
    greeted += [in_octet((member + k) % 8) for k in range(1, 8)]
    for axis, size in SIZES.items():
        for step in (1, size - 1):
            greeted.append(device({**me, axis: (me[axis] + step) % size}))
    barrier = pltpu.get_barrier_semaphore()
    for other in greeted:
        pl.semaphore_signal(barrier, inc=1, device_id=other, device_id_type=MESH)
    pl.semaphore_wait(barrier, len(greeted))

    locals_ = []

    def local_copy(src, dst):
        copy = pltpu.make_async_copy(src, dst, local_sem.at[len(locals_)])
        copy.start()
        locals_.append(copy)
        return copy

    piece_sems = [copies.new() for _ in range(7)]
    for k in range(1, 8):
        to = (member + k) % 8
        columns = pl.ds(pl.multiple_of(to * COLS, COLS), COLS)
        copies.start(
            piece_sems[k - 1],
            w_ref.at[:, columns],
            w_pieces.at[member],
            in_octet(to),
        )
    columns = pl.ds(pl.multiple_of(member * COLS, COLS), COLS)
    piece_own = local_copy(w_ref.at[:, columns], w_pieces.at[member])

    head_sems = [[copies.new() for _ in range(6)] for _ in range(7)]
    last_columns = pl.ds(LAST, HD)
    for k in range(1, 8):
        to = (local + k) % 8
        columns = pl.ds(pl.multiple_of(to * OWN, HD), OWN)
        for i, ref in enumerate((q_ref, k_ref, v_ref)):
            copies.start(
                head_sems[k - 1][i],
                ref.at[:, columns],
                qkv.at[local, i],
                in_block(to),
            )
        for i, ref in enumerate((k_ref, v_ref)):
            copies.start(
                head_sems[k - 1][3 + i],
                ref.at[:, last_columns],
                kv_last.at[local, i],
                in_block(to),
            )
        copies.start(head_sems[k - 1][5], dest_ref, dests.at[local], in_block(to))
    columns = pl.ds(pl.multiple_of(local * OWN, HD), OWN)
    head_own = [
        local_copy(ref.at[:, columns], qkv.at[local, i])
        for i, ref in enumerate((q_ref, k_ref, v_ref))
    ]
    head_own += [
        local_copy(ref.at[:, last_columns], kv_last.at[local, i])
        for i, ref in enumerate((k_ref, v_ref))
    ]
    head_own.append(local_copy(q_ref.at[:, last_columns], q_last))
    head_own.append(local_copy(dest_ref, dests.at[local]))

    piece_own.wait()
    for k in range(1, 8):
        source = (member - k + 8) % 8
        copies.arrive(piece_sems[k - 1], w_pieces.at[source], in_octet(source))
    row = lax.broadcasted_iota(jnp.int32, (ROWS, 512), 0)
    column = lax.broadcasted_iota(jnp.int32, (ROWS, 512), 1)
    inner = column % 64
    choose = one_hot((row == (column // 64) * 50 + inner) & (inner < 50))
    tile = dot(choose, w_pieces[...].reshape(512, COLS)).astype(BF)
    weight[me["y"], me["z"] // 4, me["z"] % 4, me["x"]] = tile
    gathers = [ring(copies, weight, me, part) for part in PARTS]

    def advance():
        for gather in gathers:
            next(gather, None)

    advance()

    grad_sems = [copies.new() for _ in range(2)]
    for half in range(2):
        there = pl.ds(pl.multiple_of((2 * half + 1 - core) * 2048, 2048), 2048)
        here = pl.ds(pl.multiple_of((2 * half + core) * 2048, 2048), 2048)
        into = pl.ds(half * 2048, 2048)
        copies.start(
            grad_sems[half],
            grad_ref.at[0, :, there],
            grads.at[core, :, into],
            sibling,
        )
        local_copy(grad_ref.at[0, :, here], grads.at[core, :, into])
    grad_own = locals_[-2:]

    for _ in range(6):
        advance()

    for copy in head_own:
        copy.wait()
    for k in range(1, 8):
        source = (local - k + 8) % 8
        for i in range(3):
            copies.arrive(head_sems[k - 1][i], qkv.at[source, i], in_block(source))
        for i in range(2):
            copies.arrive(
                head_sems[k - 1][3 + i], kv_last.at[source, i], in_block(source)
            )
        copies.arrive(head_sems[k - 1][5], dests.at[source], in_block(source))
    block = mp // 2
    ends = []
    total = 0
    for i in range(3):
        total = total + lengths[block, i]
        ends.append(total)
    key_segments = segments((1, BLOCK), 1, 0, ends)

    def attend_chunk(i, carry):
        columns = pl.ds(pl.multiple_of((i // 4) * HD, HD), HD)
        tiles = pl.ds((i % 4) * 2, 2)
        q = qkv[tiles, 0, :, columns].reshape(2 * TILE, HD)
        k = qkv[:, 1, :, columns].reshape(BLOCK, HD)
        v = qkv[:, 2, :, columns].reshape(BLOCK, HD)
        same = segments((2 * TILE, 1), 0, (i % 4) * 2 * TILE, ends) == key_segments
        mixed[tiles, :, columns] = attend(q, k, v, same).reshape(2, TILE, HD)
        return carry

    for head in range(3):
        lax.fori_loop(4 * head, 4 * head + 4, attend_chunk, 0)
    same = segments((TILE, 1), 0, local * TILE, ends) == key_segments
    last = attend(
        q_last[...],
        kv_last[:, 0].reshape(BLOCK, HD),
        kv_last[:, 1].reshape(BLOCK, HD),
        same,
    )
    own_placing = placing(dests[local])
    staged_last[...] = (
        dot(own_placing.astype(BF), last).astype(BF).reshape(4, CAP, HD)
    )
    last_sems = [copies.new() for _ in range(3)]
    for k in range(1, 4):
        to = (section + k) % 4
        copies.start(
            last_sems[k - 1],
            staged_last.at[to],
            slots.at[to % 2, section, :, last_columns],
            in_section(to),
        )
    last_own = local_copy(
        staged_last.at[section], slots.at[core, section, :, last_columns]
    )

    def place_tile(tile, carry):
        placed = dot(placing(dests[tile]).astype(BF), mixed[tile]).astype(BF)
        staged[tile // 4, :, tile % 4] = placed.reshape(4, CAP, OWN)
        return carry

    lax.fori_loop(0, 8, place_tile, 0)
    slot_sems = [copies.new() for _ in range(7)]
    own_columns = pl.ds(pl.multiple_of(local * OWN, HD), OWN)
    for k in range(1, 8):
        to = (local + k) % 8
        copies.start(
            slot_sems[k - 1],
            staged.at[to // 4, to % 4],
            slots.at[to % 2, :, :, own_columns],
            in_block(to),
        )
    slot_own = local_copy(
        staged.at[local // 4, local % 4], slots.at[core, :, :, own_columns]
    )
    advance()

    relay_sems = [copies.new() for _ in range(9)]

    def relay(index, columns):
        copies.start(
            relay_sems[index],
            slots.at[core, :, :, columns],
            slots.at[core, :, :, columns],
            sibling,
        )

    last_own.wait()
    for k in range(1, 4):
        source = (section - k + 4) % 4
        copies.arrive(
            last_sems[k - 1],
            slots.at[core, source, :, last_columns],
            in_section(source),
        )
    relay(8, last_columns)
    slot_own.wait()
    relay(0, own_columns)
    for k in range(1, 8):
        source = (local - k + 8) % 8
        columns = pl.ds(pl.multiple_of(source * OWN, HD), OWN)
        copies.arrive(
            slot_sems[k - 1], slots.at[core, :, :, columns], in_block(source)
        )
        relay(k, columns)
    for gather in gathers:
        for _ in gather:
            pass
    other_local = local + 1 - 2 * core
    for k in range(8):
        source = (other_local - k + 8) % 8
        columns = pl.ds(pl.multiple_of(source * OWN, HD), OWN)
        copies.arrive(relay_sems[k], slots.at[1 - core, :, :, columns], sibling)
    copies.arrive(relay_sems[8], slots.at[1 - core, :, :, last_columns], sibling)

    window_row = lax.broadcasted_iota(jnp.int32, (512, OWN), 0)
    window_column = lax.broadcasted_iota(jnp.int32, (512, OWN), 1)

    def reorder(group, carry):
        window = slots[
            :, :, :, pl.ds(pl.multiple_of(group * OWN, HD), 512)
        ].reshape(512, 512)
        moved = dot(
            window, one_hot(window_row == window_column + 16 * group)
        ).astype(BF)
        for i in range(3):
            lhs[:, pl.ds(pl.multiple_of(i * 1024 + group * HD, HD), HD)] = moved[
                :, i * HD : (i + 1) * HD
            ]
        return carry

    lax.fori_loop(0, 8, reorder, 0)
    lane = lax.broadcasted_iota(jnp.int32, (512, HD), 1) // 16
    tail = jnp.zeros((512, HD), F32)
    for group in range(8):
        piece = slots[:, :, :, OWN * (group + 1) : OWN * (group + 1) + HD]
        tail = jnp.where(lane == group, piece.reshape(512, HD).astype(F32), tail)
    lhs[:, LAST:] = tail.astype(BF)

    for copy in grad_own:
        copy.wait()
    for half in range(2):
        copies.arrive(
            grad_sems[half],
            grads.at[1 - core, :, pl.ds(half * 2048, 2048)],
            sibling,
        )
    back[...] = jnp.zeros_like(back)

    def multiply(i, carry):
        low, x = i // 4, i % 4
        column = (low % 2) * 2048 + ((low // 2) * 4 + x) * COLS
        columns = pl.ds(pl.multiple_of(column, COLS), COLS)
        grad = grads[:, :, columns].reshape(512, COLS)
        total = jnp.zeros((512, COLS), F32)
        for first, rows, start in K_PARTS:
            rhs = weight[:, :, low, x, pl.ds(first, rows), :].reshape(8 * rows, COLS)
            depth = pl.ds(start, 8 * rows)
            total = total + dot(lhs[:, depth], rhs)
            back[:, depth] += dot_nt(grad, rhs)
        embeds[:, :, columns] = total.astype(BF).reshape(2, 256, COLS)
        return carry

    embed_sems = [copies.new() for _ in range(4)]
    embed_own = []
    for low in range(4):
        lax.fori_loop(4 * low, 4 * low + 4, multiply, 0)
        half, quarter = low % 2, low // 2
        here = pl.ds(half * 2048 + quarter * 1024, 1024)
        there = pl.ds(
            pl.multiple_of((2 * half + core) * 2048 + quarter * 1024, 1024), 1024
        )
        copies.start(
            embed_sems[low],
            embeds.at[1 - core, :, here],
            embeds_ref.at[0, :, there],
            sibling,
        )
        embed_own.append(
            local_copy(embeds.at[core, :, here], embeds_ref.at[0, :, there])
        )
    copies.drain()

    half_rows = pl.ds(pl.multiple_of((1 - core) * 256, 256), 256)
    slots[0] = back[half_rows, :].astype(BF).reshape(4, CAP, DV)
    back_sem = copies.new()
    copies.start(back_sem, slots.at[0], back_in, sibling)
    copies.arrive(back_sem, back_in, sibling)
    half_rows = pl.ds(pl.multiple_of(core * 256, 256), 256)
    summed = back[half_rows, :] + back_in[...].reshape(256, DV).astype(F32)
    slots[1] = summed.astype(BF).reshape(4, CAP, DV)
    return_sems = [copies.new() for _ in range(3)]
    for k in range(1, 4):
        to = (section + k) % 4
        copies.start(
            return_sems[k - 1], slots.at[1, to], returned.at[section], in_section(to)
        )
    local_copy(slots.at[1, section], returned.at[section]).wait()
    for k in range(1, 4):
        source = (section - k + 4) % 4
        copies.arrive(return_sems[k - 1], returned.at[source], in_section(source))
    chosen = dot(
        own_placing.T.astype(BF), returned[...].reshape(256, DV)
    ).astype(BF)
    rows = pl.ds(0, TILE)
    back[rows, :] = jnp.zeros((TILE, DV), F32)
    lane = lax.broadcasted_iota(jnp.int32, (TILE, HD), 1) // 16
    tail = chosen[:, LAST:].astype(F32)
    source_lane = lax.broadcasted_iota(jnp.int32, (OWN, 512), 0)
    target_lane = lax.broadcasted_iota(jnp.int32, (OWN, 512), 1)
    for group in range(8):
        piece = jnp.concatenate(
            [chosen[:, i * 1024 + group * HD : i * 1024 + (group + 1) * HD] for i in range(3)],
            axis=1,
        )
        moved = dot(piece, one_hot(target_lane == source_lane + 16 * group))
        back[rows, group * OWN : group * OWN + 512] += moved
        back[rows, (group + 1) * OWN : (group + 1) * OWN + HD] += jnp.where(
            lane == group, tail, 0.0
        )
    vgrad_ref[...] = back[rows, :].astype(BF)

    for copy in embed_own:
        copy.wait()
    for low in range(4):
        half, quarter = low % 2, low // 2
        there = pl.ds(
            pl.multiple_of((2 * half + 1 - core) * 2048 + quarter * 1024, 1024), 1024
        )
        copies.arrive(embed_sems[low], embeds_ref.at[0, :, there], sibling)
    copies.drain()


def on_device(query_rows, key_rows, value_rows, image_lengths, dest_group, proj_weight, llm_grad):
    dest = jnp.broadcast_to(dest_group.reshape(1, TILE), (8, TILE))
    shard = jnp.pad(proj_weight, ((0, 64 - proj_weight.shape[0]), (0, 0)))
    any_ = pl.BlockSpec(memory_space=pl.ANY)
    vmem = pltpu.VMEM
    return pl.pallas_call(
        kernel,
        out_shape=(
            jax.ShapeDtypeStruct(llm_grad.shape, BF),
            jax.ShapeDtypeStruct(query_rows.shape, BF),
        ),
        in_specs=[pl.BlockSpec(memory_space=pltpu.SMEM)] + [any_] * 6,
        out_specs=(any_, pl.BlockSpec(memory_space=pltpu.VMEM)),
        scratch_shapes=[
            vmem((4, 2, 4, 4, ROWS, COLS), BF),
            vmem((8, 64, COLS), BF),
            vmem((8, 3, TILE, OWN), BF),
            vmem((8, 2, TILE, HD), BF),
            vmem((TILE, HD), BF),
            vmem((8, 8, TILE), jnp.int32),
            vmem((8, TILE, OWN), BF),
            vmem((2, 4, 4, CAP, OWN), BF),
            vmem((4, CAP, HD), BF),
            vmem((2, 4, CAP, DV), BF),
            vmem((512, DV), BF),
            vmem((2, 256, 4096), BF),
            vmem((2, 256, 4096), BF),
            vmem((512, DV), F32),
            vmem((4, CAP, DV), BF),
            vmem((4, CAP, DV), BF),
            pltpu.SemaphoreType.DMA((192,)),
            pltpu.SemaphoreType.DMA((192,)),
            pltpu.SemaphoreType.DMA((32,)),
        ],
        compiler_params=pltpu.CompilerParams(
            collective_id=0, has_side_effects=True, vmem_limit_bytes=64 * 1024 * 1024
        ),
    )(image_lengths, dest, query_rows, key_rows, value_rows, shard, llm_grad)


def solution(mesh):
    placed = (
        P(("mp", "section"), None),
        P(("mp", "section"), None),
        P(("mp", "section"), None),
        P(),
        P(("mp", "section"), None),
        P("mp", "section"),
        P("section", "mp", None),
    )
    return jax.shard_map(
        on_device,
        mesh=mesh,
        in_specs=placed,
        out_specs=(P("section", "mp", None), P(("mp", "section"), None)),
        check_vma=False,
    )
```

```python
import functools

import jax
import jax.numpy as jnp
from jax import lax
from jax.experimental import pallas as pl
from jax.experimental.pallas import tpu as pltpu
from jax.sharding import PartitionSpec as P

MESH = pl.DeviceIdType.MESH
BF = jnp.bfloat16
F32 = jnp.float32
HD = 128
BLOCK = 1024
TILE = 128
CAP = 64
DV = 3200
OWN = 384
LAST = 3072
ROWS = 400
COLS = 256
SIZES = {"x": 4, "y": 4, "z": 8}
PARTS = (
    (0, 48, "xyz", 0),
    (48, 48, "xyz", 0),
    (96, 32, "zxy", 1),
    (128, 64, "zyx", 0),
    (192, 64, "zyx", 0),
    (256, 80, "zxy", 0),
    (336, 64, "zxy", 1),
)
K_PARTS = ((0, 128, 0), (128, 128, 1024), (256, 128, 2048), (384, 16, 3072))


def place():
    section, mp = lax.axis_index("section"), lax.axis_index("mp")
    return {
        "x": mp % 4,
        "y": mp // 16,
        "z": ((mp // 4) % 4) * 2 + section // 2,
        "c": section % 2,
    }


def device(at):
    return {
        "mp": (at["y"] * 4 + at["z"] // 2) * 4 + at["x"],
        "section": (at["z"] % 2) * 2 + at["c"],
    }


def one_hot(condition):
    return jnp.where(condition, 1.0, 0.0).astype(BF)


def dot(a, b):
    return jnp.dot(a, b, preferred_element_type=F32)


def dot_nt(a, b):
    return lax.dot_general(a, b, (((1,), (1,)), ((), ())), preferred_element_type=F32)


def placing(dest):
    group = lax.broadcasted_iota(jnp.int32, (8, TILE), 0)
    named = jnp.where(group == dest, 1.0, 0.0)
    before = one_hot(
        lax.broadcasted_iota(jnp.int32, (TILE, TILE), 0)
        < lax.broadcasted_iota(jnp.int32, (TILE, TILE), 1)
    )
    earlier = dot(named.astype(BF), before)
    rank = jnp.sum(named * earlier, axis=0, keepdims=True)
    target = dest[0:1].astype(F32) * float(CAP) + rank
    slots = lax.broadcasted_iota(jnp.int32, (4 * CAP, TILE), 0).astype(F32)
    return jnp.where(slots == target, 1.0, 0.0)


def segments(shape, axis, start, ends):
    rows = lax.broadcasted_iota(jnp.int32, shape, axis) + start
    count = jnp.zeros(shape, jnp.int32)
    for end in ends:
        count = count + jnp.where(rows >= end, 1, 0)
    return count


def attend(q, k, v, same):
    scores = dot_nt(q, k) * HD ** (-0.5)
    scores = jnp.where(same, scores, -1e30)
    raised = jnp.exp(scores - jnp.max(scores, axis=1, keepdims=True))
    inverse = 1.0 / jnp.sum(raised, axis=1, keepdims=True)
    return dot((raised * inverse).astype(BF), v).astype(BF)


class Copies:
    def __init__(self, send, recv):
        self.send, self.recv, self.count, self.sent = send, recv, 0, []

    def new(self):
        self.count += 1
        return self.count - 1

    def make(self, index, src, dst, to):
        return pltpu.make_async_remote_copy(
            src_ref=src,
            dst_ref=dst,
            send_sem=self.send.at[index],
            recv_sem=self.recv.at[index],
            device_id=to,
            device_id_type=MESH,
        )

    def start(self, index, src, dst, to):
        copy = self.make(index, src, dst, to)
        copy.start()
        self.sent.append(copy)
        return copy

    def arrive(self, index, dst, to):
        self.make(index, dst, dst, to).wait_recv()

    def drain(self):
        for copy in self.sent:
            copy.wait_send()
        self.sent = []


def ring(copies, buf, me, part):
    first, rows, order, flip = part
    done = []
    for axis in order:
        size = SIZES[axis]
        even = 1 - 2 * (me[axis] % 2)
        if not done:
            def tile_at(offset):
                at = {a: me[a] for a in SIZES}
                at[axis] = (me[axis] + offset * even + size) % size
                spot = (at["y"], at["z"] // 4, at["z"] % 4, at["x"])
                return buf.at[(*spot, pl.ds(first, rows), slice(None))], device(
                    {**me, axis: at[axis]}
                )

            indices = [copies.new() for _ in range(size)]
            for offset in range(1, size):
                copies.start(
                    indices[offset], tile_at(0)[0], tile_at(0)[0], tile_at(offset)[1]
                )
            yield
            for offset in range(1, size):
                index = indices[offset if offset % 2 else size - offset]
                copies.arrive(index, *tile_at(offset))
            done = [axis]
            continue
        step = -even if flip else even
        near = {**me, axis: (me[axis] + step + size) % size}
        far = {**me, axis: (me[axis] - step + size) % size}

        def block(offset):
            at = {
                **{a: me[a] for a in SIZES},
                axis: (me[axis] + offset * step + size) % size,
            }
            index = []
            for a in ("y", "z", "x"):
                if a in done:
                    index += [slice(None)] * (2 if a == "z" else 1)
                elif a == "z":
                    index += [at[a] // 4, at[a] % 4]
                else:
                    index += [at[a]]
            return buf.at[(*index, pl.ds(first, rows), slice(None))]

        to_far = [copies.new() for _ in range(size // 2)]
        to_near = [copies.new() for _ in range(size // 2 - 1)]
        copies.start(to_far[0], block(0), block(0), device(far))
        copies.start(to_near[0], block(0), block(0), device(near))
        for k in range(size // 2):
            yield
            if k < size // 2 - 1:
                copies.arrive(to_near[k], block(k + 1), device(near))
                copies.start(to_far[k + 1], block(k + 1), block(k + 1), device(far))
            copies.arrive(to_far[k], block(-(k + 1)), device(far))
            if k + 1 < size // 2 - 1:
                copies.start(
                    to_near[k + 1], block(-(k + 1)), block(-(k + 1)), device(near)
                )
        done = done + [axis]


def kernel(
    lengths,
    dest_col,
    q_ref,
    k_ref,
    v_ref,
    w_rows,
    grad_ref,
    embeds_ref,
    vgrad_ref,
    w_ref,
    dest_ref,
    weight,
    w_pieces,
    qkv,
    kv_last,
    q_last,
    dests,
    mixed,
    staged,
    staged_last,
    slots,
    lhs,
    grads,
    embeds,
    back,
    back_in,
    returned,
    send_sem,
    recv_sem,
    local_sem,
):
    me = place()
    section, mp = lax.axis_index("section"), lax.axis_index("mp")
    core = me["c"]
    local = (mp % 2) * 4 + section
    member = mp % 8
    copies = Copies(send_sem, recv_sem)
    sibling = device({**me, "c": 1 - core})

    def in_block(index):
        return {"mp": mp - mp % 2 + index // 4, "section": index % 4}

    def in_octet(index):
        return {"mp": mp - mp % 8 + index, "section": section}

    def in_section(index):
        return {"mp": mp, "section": index}

    greeted = [in_block((local + k) % 8) for k in range(1, 8)]
    greeted += [in_octet((member + k) % 8) for k in range(1, 8)]
    for axis, size in SIZES.items():
        for step in range(1, size):
            greeted.append(device({**me, axis: (me[axis] + step) % size}))
    barrier = pltpu.get_barrier_semaphore()
    for other in greeted:
        pl.semaphore_signal(barrier, inc=1, device_id=other, device_id_type=MESH)
    across = lax.broadcasted_iota(jnp.int32, (64, 50), 1)
    down = lax.broadcasted_iota(jnp.int32, (64, 50), 0)
    w_ref[...] = dot(one_hot(across == down), w_rows[...]).astype(BF)
    diagonal = lax.broadcasted_iota(jnp.int32, (TILE, TILE), 0) == (
        lax.broadcasted_iota(jnp.int32, (TILE, TILE), 1)
    )
    turned = jnp.sum(
        jnp.where(diagonal, dest_col[...].astype(F32), 0.0), axis=0, keepdims=True
    )
    dest_ref[...] = jnp.broadcast_to(turned, (8, TILE)).astype(jnp.int32)
    pl.semaphore_wait(barrier, len(greeted))

    locals_ = []

    def local_copy(src, dst):
        copy = pltpu.make_async_copy(src, dst, local_sem.at[len(locals_)])
        copy.start()
        locals_.append(copy)
        return copy

    piece_sems = [copies.new() for _ in range(7)]
    for k in range(1, 8):
        to = (member + k) % 8
        columns = pl.ds(pl.multiple_of(to * COLS, COLS), COLS)
        copies.start(
            piece_sems[k - 1],
            w_ref.at[:, columns],
            w_pieces.at[member],
            in_octet(to),
        )
    columns = pl.ds(pl.multiple_of(member * COLS, COLS), COLS)
    piece_own = local_copy(w_ref.at[:, columns], w_pieces.at[member])

    head_sems = [[copies.new() for _ in range(6)] for _ in range(7)]
    last_columns = pl.ds(LAST, HD)
    for k in range(1, 8):
        to = (local + k) % 8
        columns = pl.ds(pl.multiple_of(to * OWN, HD), OWN)
        for i, ref in enumerate((q_ref, k_ref, v_ref)):
            copies.start(
                head_sems[k - 1][i],
                ref.at[:, columns],
                qkv.at[local, i],
                in_block(to),
            )
        for i, ref in enumerate((k_ref, v_ref)):
            copies.start(
                head_sems[k - 1][3 + i],
                ref.at[:, last_columns],
                kv_last.at[local, i],
                in_block(to),
            )
        copies.start(head_sems[k - 1][5], dest_ref, dests.at[local], in_block(to))
    columns = pl.ds(pl.multiple_of(local * OWN, HD), OWN)
    head_own = [
        local_copy(ref.at[:, columns], qkv.at[local, i])
        for i, ref in enumerate((q_ref, k_ref, v_ref))
    ]
    head_own += [
        local_copy(ref.at[:, last_columns], kv_last.at[local, i])
        for i, ref in enumerate((k_ref, v_ref))
    ]
    head_own.append(local_copy(q_ref.at[:, last_columns], q_last))
    head_own.append(local_copy(dest_ref, dests.at[local]))

    piece_own.wait()
    for k in range(1, 8):
        source = (member - k + 8) % 8
        copies.arrive(piece_sems[k - 1], w_pieces.at[source], in_octet(source))
    row = lax.broadcasted_iota(jnp.int32, (ROWS, 512), 0)
    column = lax.broadcasted_iota(jnp.int32, (ROWS, 512), 1)
    inner = column % 64
    choose = one_hot((row == (column // 64) * 50 + inner) & (inner < 50))
    tile = dot(choose, w_pieces[...].reshape(512, COLS)).astype(BF)
    weight[me["y"], me["z"] // 4, me["z"] % 4, me["x"]] = tile
    gathers = [ring(copies, weight, me, part) for part in PARTS]

    def advance():
        for gather in gathers:
            next(gather, None)

    advance()

    grad_sems = [copies.new() for _ in range(2)]
    for half in range(2):
        there = pl.ds(pl.multiple_of((2 * half + 1 - core) * 2048, 2048), 2048)
        here = pl.ds(pl.multiple_of((2 * half + core) * 2048, 2048), 2048)
        into = pl.ds(half * 2048, 2048)
        copies.start(
            grad_sems[half],
            grad_ref.at[0, :, there],
            grads.at[core, :, into],
            sibling,
        )
        local_copy(grad_ref.at[0, :, here], grads.at[core, :, into])
    grad_own = locals_[-2:]

    for _ in range(3):
        advance()

    for copy in head_own:
        copy.wait()
    for k in range(1, 8):
        source = (local - k + 8) % 8
        for i in range(3):
            copies.arrive(head_sems[k - 1][i], qkv.at[source, i], in_block(source))
        for i in range(2):
            copies.arrive(
                head_sems[k - 1][3 + i], kv_last.at[source, i], in_block(source)
            )
        copies.arrive(head_sems[k - 1][5], dests.at[source], in_block(source))
    block = mp // 2
    ends = []
    total = 0
    for i in range(3):
        total = total + lengths[i, block]
        ends.append(total)
    key_segments = segments((1, BLOCK), 1, 0, ends)

    def attend_chunk(i, carry):
        columns = pl.ds(pl.multiple_of((i // 4) * HD, HD), HD)
        tiles = pl.ds((i % 4) * 2, 2)
        q = qkv[tiles, 0, :, columns].reshape(2 * TILE, HD)
        k = qkv[:, 1, :, columns].reshape(BLOCK, HD)
        v = qkv[:, 2, :, columns].reshape(BLOCK, HD)
        same = segments((2 * TILE, 1), 0, (i % 4) * 2 * TILE, ends) == key_segments
        mixed[tiles, :, columns] = attend(q, k, v, same).reshape(2, TILE, HD)
        return carry

    def advance_z():
        for gather in gathers[:2]:
            next(gather, None)

    advance_z()
    for head in range(3):
        lax.fori_loop(4 * head, 4 * head + 4, attend_chunk, 0)
    advance_z()
    same = segments((TILE, 1), 0, local * TILE, ends) == key_segments
    last = attend(
        q_last[...],
        kv_last[:, 0].reshape(BLOCK, HD),
        kv_last[:, 1].reshape(BLOCK, HD),
        same,
    )
    own_placing = placing(dests[local])
    staged_last[...] = (
        dot(own_placing.astype(BF), last).astype(BF).reshape(4, CAP, HD)
    )
    last_sems = [copies.new() for _ in range(3)]
    for k in range(1, 4):
        to = (section + k) % 4
        copies.start(
            last_sems[k - 1],
            staged_last.at[to],
            slots.at[to % 2, section, :, last_columns],
            in_section(to),
        )
    last_own = local_copy(
        staged_last.at[section], slots.at[core, section, :, last_columns]
    )

    def place_tile(tile, carry):
        placed = dot(placing(dests[tile]).astype(BF), mixed[tile]).astype(BF)
        staged[tile // 4, :, tile % 4] = placed.reshape(4, CAP, OWN)
        return carry

    lax.fori_loop(0, 8, place_tile, 0)
    slot_sems = [copies.new() for _ in range(7)]
    own_columns = pl.ds(pl.multiple_of(local * OWN, HD), OWN)
    for k in range(1, 8):
        to = (local + k) % 8
        copies.start(
            slot_sems[k - 1],
            staged.at[to // 4, to % 4],
            slots.at[to % 2, :, :, own_columns],
            in_block(to),
        )
    slot_own = local_copy(
        staged.at[local // 4, local % 4], slots.at[core, :, :, own_columns]
    )
    advance()

    relay_sems = [copies.new() for _ in range(9)]

    def relay(index, columns):
        copies.start(
            relay_sems[index],
            slots.at[core, :, :, columns],
            slots.at[core, :, :, columns],
            sibling,
        )

    last_own.wait()
    for k in range(1, 4):
        source = (section - k + 4) % 4
        copies.arrive(
            last_sems[k - 1],
            slots.at[core, source, :, last_columns],
            in_section(source),
        )
    relay(8, last_columns)
    slot_own.wait()
    relay(0, own_columns)
    for k in range(1, 8):
        source = (local - k + 8) % 8
        columns = pl.ds(pl.multiple_of(source * OWN, HD), OWN)
        copies.arrive(
            slot_sems[k - 1], slots.at[core, :, :, columns], in_block(source)
        )
        relay(k, columns)
    for gather in gathers:
        for _ in gather:
            pass
    other_local = local + 1 - 2 * core
    for k in range(8):
        source = (other_local - k + 8) % 8
        columns = pl.ds(pl.multiple_of(source * OWN, HD), OWN)
        copies.arrive(relay_sems[k], slots.at[1 - core, :, :, columns], sibling)
    copies.arrive(relay_sems[8], slots.at[1 - core, :, :, last_columns], sibling)

    window_row = lax.broadcasted_iota(jnp.int32, (512, OWN), 0)
    window_column = lax.broadcasted_iota(jnp.int32, (512, OWN), 1)

    def reorder(group, carry):
        window = slots[
            :, :, :, pl.ds(pl.multiple_of(group * OWN, HD), 512)
        ].reshape(512, 512)
        moved = dot(
            window, one_hot(window_row == window_column + 16 * group)
        ).astype(BF)
        for i in range(3):
            lhs[:, pl.ds(pl.multiple_of(i * 1024 + group * HD, HD), HD)] = moved[
                :, i * HD : (i + 1) * HD
            ]
        return carry

    lax.fori_loop(0, 8, reorder, 0)
    lane = lax.broadcasted_iota(jnp.int32, (512, HD), 1) // 16
    tail = jnp.zeros((512, HD), F32)
    for group in range(8):
        piece = slots[:, :, :, OWN * (group + 1) : OWN * (group + 1) + HD]
        tail = jnp.where(lane == group, piece.reshape(512, HD).astype(F32), tail)
    lhs[:, LAST:] = tail.astype(BF)

    for copy in grad_own:
        copy.wait()
    for half in range(2):
        copies.arrive(
            grad_sems[half],
            grads.at[1 - core, :, pl.ds(half * 2048, 2048)],
            sibling,
        )
    back[...] = jnp.zeros_like(back)

    def chunk(i):
        low, x = i // 4, i % 4
        column = (low % 2) * 2048 + ((low // 2) * 4 + x) * COLS
        columns = pl.ds(pl.multiple_of(column, COLS), COLS)
        return low, x, columns

    def weight_rows(first, rows, low, x):
        return weight[:, :, low, x, pl.ds(first, rows), :].reshape(8 * rows, COLS)

    def multiply_back(i, carry):
        low, x, columns = chunk(i)
        grad = grads[:, :, columns].reshape(512, COLS)
        for first, rows, start in K_PARTS:
            back[:, pl.ds(start, 8 * rows)] += dot_nt(
                grad, weight_rows(first, rows, low, x)
            )
        return carry

    def multiply(i, carry):
        low, x, columns = chunk(i)
        total = jnp.zeros((512, COLS), F32)
        for first, rows, start in K_PARTS:
            total = total + dot(
                lhs[:, pl.ds(start, 8 * rows)], weight_rows(first, rows, low, x)
            )
        embeds[:, :, columns] = total.astype(BF).reshape(2, 256, COLS)
        return carry

    copies.drain()
    lax.fori_loop(0, 16, multiply_back, 0)

    half_rows = pl.ds(pl.multiple_of((1 - core) * 256, 256), 256)
    slots[0] = back[half_rows, :].astype(BF).reshape(4, CAP, DV)
    back_sem = copies.new()
    copies.start(back_sem, slots.at[0], back_in, sibling)
    return_sems = [copies.new() for _ in range(3)]
    returned_own = []

    def add_back():
        copies.arrive(back_sem, back_in, sibling)
        half_rows = pl.ds(pl.multiple_of(core * 256, 256), 256)
        summed = back[half_rows, :] + back_in[...].reshape(256, DV).astype(F32)
        slots[1] = summed.astype(BF).reshape(4, CAP, DV)
        for k in range(1, 4):
            to = (section + k) % 4
            copies.start(
                return_sems[k - 1],
                slots.at[1, to],
                returned.at[section],
                in_section(to),
            )
        returned_own.append(local_copy(slots.at[1, section], returned.at[section]))

    embed_sems = [copies.new() for _ in range(4)]
    embed_own = []
    for low in range(4):
        lax.fori_loop(4 * low, 4 * low + 4, multiply, 0)
        if low == 1:
            add_back()
        half, quarter = low % 2, low // 2
        here = pl.ds(half * 2048 + quarter * 1024, 1024)
        there = pl.ds(
            pl.multiple_of((2 * half + core) * 2048 + quarter * 1024, 1024), 1024
        )
        copies.start(
            embed_sems[low],
            embeds.at[1 - core, :, here],
            embeds_ref.at[0, :, there],
            sibling,
        )
        embed_own.append(
            local_copy(embeds.at[core, :, here], embeds_ref.at[0, :, there])
        )
    returned_own[0].wait()
    for k in range(1, 4):
        source = (section - k + 4) % 4
        copies.arrive(return_sems[k - 1], returned.at[source], in_section(source))
    chosen = dot(
        own_placing.T.astype(BF), returned[...].reshape(256, DV)
    ).astype(BF)
    rows = pl.ds(0, TILE)
    back[rows, :] = jnp.zeros((TILE, DV), F32)
    lane = lax.broadcasted_iota(jnp.int32, (TILE, HD), 1) // 16
    tail = chosen[:, LAST:].astype(F32)
    source_lane = lax.broadcasted_iota(jnp.int32, (OWN, 512), 0)
    target_lane = lax.broadcasted_iota(jnp.int32, (OWN, 512), 1)
    for group in range(8):
        piece = jnp.concatenate(
            [chosen[:, i * 1024 + group * HD : i * 1024 + (group + 1) * HD] for i in range(3)],
            axis=1,
        )
        moved = dot(piece, one_hot(target_lane == source_lane + 16 * group))
        back[rows, group * OWN : group * OWN + 512] += moved
        back[rows, (group + 1) * OWN : (group + 1) * OWN + HD] += jnp.where(
            lane == group, tail, 0.0
        )
    vgrad_ref[...] = back[rows, :].astype(BF)

    for copy in embed_own:
        copy.wait()
    for low in range(4):
        half, quarter = low % 2, low // 2
        there = pl.ds(
            pl.multiple_of((2 * half + 1 - core) * 2048 + quarter * 1024, 1024), 1024
        )
        copies.arrive(embed_sems[low], embeds_ref.at[0, :, there], sibling)
    copies.drain()


def on_device(query_rows, key_rows, value_rows, image_lengths, dest_group, proj_weight, llm_grad):
    any_ = pl.BlockSpec(memory_space=pl.ANY)
    in_vmem = pl.BlockSpec(memory_space=pltpu.VMEM)
    vmem = pltpu.VMEM
    return pl.pallas_call(
        kernel,
        out_shape=(
            jax.ShapeDtypeStruct(llm_grad.shape, BF),
            jax.ShapeDtypeStruct(query_rows.shape, BF),
        ),
        in_specs=[pl.BlockSpec(memory_space=pltpu.SMEM), in_vmem, any_, any_, any_, in_vmem, any_],
        out_specs=(any_, pl.BlockSpec(memory_space=pltpu.VMEM)),
        scratch_shapes=[
            vmem((64, 2048), BF),
            vmem((8, TILE), jnp.int32),
            vmem((4, 2, 4, 4, ROWS, COLS), BF),
            vmem((8, 64, COLS), BF),
            vmem((8, 3, TILE, OWN), BF),
            vmem((8, 2, TILE, HD), BF),
            vmem((TILE, HD), BF),
            vmem((8, 8, TILE), jnp.int32),
            vmem((8, TILE, OWN), BF),
            vmem((2, 4, 4, CAP, OWN), BF),
            vmem((4, CAP, HD), BF),
            vmem((2, 4, CAP, DV), BF),
            vmem((512, DV), BF),
            vmem((2, 256, 4096), BF),
            vmem((2, 256, 4096), BF),
            vmem((512, DV), F32),
            vmem((4, CAP, DV), BF),
            vmem((4, CAP, DV), BF),
            pltpu.SemaphoreType.DMA((192,)),
            pltpu.SemaphoreType.DMA((192,)),
            pltpu.SemaphoreType.DMA((32,)),
        ],
        compiler_params=pltpu.CompilerParams(
            collective_id=0, has_side_effects=True, vmem_limit_bytes=64 * 1024 * 1024
        ),
    )(image_lengths.T, dest_group, query_rows, key_rows, value_rows, proj_weight, llm_grad)


def solution(mesh):
    placed = (
        P(("mp", "section"), None),
        P(("mp", "section"), None),
        P(("mp", "section"), None),
        P(),
        P(("mp", "section"), None),
        P("mp", "section"),
        P("section", "mp", None),
    )
    return jax.shard_map(
        on_device,
        mesh=mesh,
        in_specs=placed,
        out_specs=(P("section", "mp", None), P(("mp", "section"), None)),
        check_vma=False,
    )
```

```python
import functools

import jax
import jax.numpy as jnp
from jax import lax
from jax.experimental import pallas as pl
from jax.experimental.pallas import tpu as pltpu
from jax.sharding import PartitionSpec as P

MESH = pl.DeviceIdType.MESH
BF = jnp.bfloat16
F32 = jnp.float32
HD = 128
BLOCK = 1024
TILE = 128
CAP = 64
DV = 3200
OWN = 384
LAST = 3072
ROWS = 400
COLS = 256
SIZES = {"x": 4, "y": 4, "z": 8}
PARTS = (
    (0, 48, "xyz", 0),
    (48, 48, "xyz", 0),
    (96, 32, "zxy", 1),
    (128, 64, "zyx", 0),
    (192, 64, "zyx", 0),
    (256, 80, "zxy", 0),
    (336, 64, "zxy", 1),
)
K_PARTS = ((0, 128, 0), (128, 128, 1024), (256, 128, 2048), (384, 16, 3072))


def place():
    section, mp = lax.axis_index("section"), lax.axis_index("mp")
    return {
        "x": mp % 4,
        "y": mp // 16,
        "z": ((mp // 4) % 4) * 2 + section // 2,
        "c": section % 2,
    }


def device(at):
    return {
        "mp": (at["y"] * 4 + at["z"] // 2) * 4 + at["x"],
        "section": (at["z"] % 2) * 2 + at["c"],
    }


def one_hot(condition):
    return jnp.where(condition, 1.0, 0.0).astype(BF)


def dot(a, b):
    return jnp.dot(a, b, preferred_element_type=F32)


def dot_nt(a, b):
    return lax.dot_general(a, b, (((1,), (1,)), ((), ())), preferred_element_type=F32)


def placing(dest):
    group = lax.broadcasted_iota(jnp.int32, (8, TILE), 0)
    named = jnp.where(group == dest, 1.0, 0.0)
    before = one_hot(
        lax.broadcasted_iota(jnp.int32, (TILE, TILE), 0)
        < lax.broadcasted_iota(jnp.int32, (TILE, TILE), 1)
    )
    earlier = dot(named.astype(BF), before)
    rank = jnp.sum(named * earlier, axis=0, keepdims=True)
    target = dest[0:1].astype(F32) * float(CAP) + rank
    slots = lax.broadcasted_iota(jnp.int32, (4 * CAP, TILE), 0).astype(F32)
    return jnp.where(slots == target, 1.0, 0.0)


def segments(shape, axis, start, ends):
    rows = lax.broadcasted_iota(jnp.int32, shape, axis) + start
    count = jnp.zeros(shape, jnp.int32)
    for end in ends:
        count = count + jnp.where(rows >= end, 1, 0)
    return count


def attend(q, k, v, same):
    scores = dot_nt(q, k) * HD ** (-0.5)
    scores = jnp.where(same, scores, -1e30)
    raised = jnp.exp(scores - jnp.max(scores, axis=1, keepdims=True))
    inverse = 1.0 / jnp.sum(raised, axis=1, keepdims=True)
    return dot((raised * inverse).astype(BF), v).astype(BF)


class Copies:
    def __init__(self, send, recv):
        self.send, self.recv, self.count, self.sent = send, recv, 0, []

    def new(self):
        self.count += 1
        return self.count - 1

    def make(self, index, src, dst, to):
        return pltpu.make_async_remote_copy(
            src_ref=src,
            dst_ref=dst,
            send_sem=self.send.at[index],
            recv_sem=self.recv.at[index],
            device_id=to,
            device_id_type=MESH,
        )

    def start(self, index, src, dst, to):
        copy = self.make(index, src, dst, to)
        copy.start()
        self.sent.append(copy)
        return copy

    def arrive(self, index, dst, to):
        self.make(index, dst, dst, to).wait_recv()

    def drain(self):
        for copy in self.sent:
            copy.wait_send()
        self.sent = []


def ring(copies, buf, me, part):
    first, rows, order, flip = part
    done = []
    for axis in order:
        size = SIZES[axis]
        even = 1 - 2 * (me[axis] % 2)
        if not done:
            def tile_at(offset):
                at = {a: me[a] for a in SIZES}
                at[axis] = (me[axis] + offset * even + size) % size
                spot = (at["y"], at["z"] // 4, at["z"] % 4, at["x"])
                return buf.at[(*spot, pl.ds(first, rows), slice(None))], device(
                    {**me, axis: at[axis]}
                )

            indices = [copies.new() for _ in range(size)]
            for offset in range(1, size):
                copies.start(
                    indices[offset], tile_at(0)[0], tile_at(0)[0], tile_at(offset)[1]
                )
            yield
            for offset in range(1, size):
                index = indices[offset if offset % 2 else size - offset]
                copies.arrive(index, *tile_at(offset))
            done = [axis]
            continue
        step = -even if flip else even
        near = {**me, axis: (me[axis] + step + size) % size}
        far = {**me, axis: (me[axis] - step + size) % size}

        def block(offset):
            at = {
                **{a: me[a] for a in SIZES},
                axis: (me[axis] + offset * step + size) % size,
            }
            index = []
            for a in ("y", "z", "x"):
                if a in done:
                    index += [slice(None)] * (2 if a == "z" else 1)
                elif a == "z":
                    index += [at[a] // 4, at[a] % 4]
                else:
                    index += [at[a]]
            return buf.at[(*index, pl.ds(first, rows), slice(None))]

        to_far = [copies.new() for _ in range(size // 2)]
        to_near = [copies.new() for _ in range(size // 2 - 1)]
        copies.start(to_far[0], block(0), block(0), device(far))
        copies.start(to_near[0], block(0), block(0), device(near))
        for k in range(size // 2):
            yield
            if k < size // 2 - 1:
                copies.arrive(to_near[k], block(k + 1), device(near))
                copies.start(to_far[k + 1], block(k + 1), block(k + 1), device(far))
            copies.arrive(to_far[k], block(-(k + 1)), device(far))
            if k + 1 < size // 2 - 1:
                copies.start(
                    to_near[k + 1], block(-(k + 1)), block(-(k + 1)), device(near)
                )
        done = done + [axis]


def kernel(
    lengths,
    dest_col,
    q_ref,
    k_ref,
    v_ref,
    w_rows,
    grad_ref,
    embeds_ref,
    vgrad_ref,
    w_ref,
    dest_ref,
    weight,
    w_pieces,
    qkv,
    kv_last,
    q_last,
    dests,
    mixed,
    staged,
    staged_last,
    slots,
    lhs,
    grads,
    embeds,
    back,
    back_in,
    returned,
    send_sem,
    recv_sem,
    local_sem,
):
    me = place()
    section, mp = lax.axis_index("section"), lax.axis_index("mp")
    core = me["c"]
    local = (mp % 2) * 4 + section
    member = mp % 8
    copies = Copies(send_sem, recv_sem)
    sibling = device({**me, "c": 1 - core})

    def in_block(index):
        return {"mp": mp - mp % 2 + index // 4, "section": index % 4}

    def in_octet(index):
        return {"mp": mp - mp % 8 + index, "section": section}

    def in_section(index):
        return {"mp": mp, "section": index}

    greeted = [in_block((local + k) % 8) for k in range(1, 8)]
    greeted += [in_octet((member + k) % 8) for k in range(1, 8)]
    for axis, size in SIZES.items():
        for step in range(1, size):
            greeted.append(device({**me, axis: (me[axis] + step) % size}))
    barrier = pltpu.get_barrier_semaphore()
    for other in greeted:
        pl.semaphore_signal(barrier, inc=1, device_id=other, device_id_type=MESH)
    across = lax.broadcasted_iota(jnp.int32, (64, 50), 1)
    down = lax.broadcasted_iota(jnp.int32, (64, 50), 0)
    w_ref[...] = dot(one_hot(across == down), w_rows[...]).astype(BF)
    diagonal = lax.broadcasted_iota(jnp.int32, (TILE, TILE), 0) == (
        lax.broadcasted_iota(jnp.int32, (TILE, TILE), 1)
    )
    turned = jnp.sum(
        jnp.where(diagonal, dest_col[...].astype(F32), 0.0), axis=0, keepdims=True
    )
    dest_ref[...] = jnp.broadcast_to(turned, (8, TILE)).astype(jnp.int32)
    pl.semaphore_wait(barrier, len(greeted))

    locals_ = []

    def local_copy(src, dst):
        copy = pltpu.make_async_copy(src, dst, local_sem.at[len(locals_)])
        copy.start()
        locals_.append(copy)
        return copy

    piece_sems = [copies.new() for _ in range(7)]
    for k in range(1, 8):
        to = (member + k) % 8
        columns = pl.ds(pl.multiple_of(to * COLS, COLS), COLS)
        copies.start(
            piece_sems[k - 1],
            w_ref.at[:, columns],
            w_pieces.at[member],
            in_octet(to),
        )
    columns = pl.ds(pl.multiple_of(member * COLS, COLS), COLS)
    piece_own = local_copy(w_ref.at[:, columns], w_pieces.at[member])

    head_sems = [[copies.new() for _ in range(6)] for _ in range(7)]
    last_columns = pl.ds(LAST, HD)
    for k in range(1, 8):
        to = (local + k) % 8
        columns = pl.ds(pl.multiple_of(to * OWN, HD), OWN)
        for i, ref in enumerate((q_ref, k_ref, v_ref)):
            copies.start(
                head_sems[k - 1][i],
                ref.at[:, columns],
                qkv.at[local, i],
                in_block(to),
            )
        for i, ref in enumerate((k_ref, v_ref)):
            copies.start(
                head_sems[k - 1][3 + i],
                ref.at[:, last_columns],
                kv_last.at[local, i],
                in_block(to),
            )
        copies.start(head_sems[k - 1][5], dest_ref, dests.at[local], in_block(to))
    columns = pl.ds(pl.multiple_of(local * OWN, HD), OWN)
    head_own = [
        local_copy(ref.at[:, columns], qkv.at[local, i])
        for i, ref in enumerate((q_ref, k_ref, v_ref))
    ]
    head_own += [
        local_copy(ref.at[:, last_columns], kv_last.at[local, i])
        for i, ref in enumerate((k_ref, v_ref))
    ]
    head_own.append(local_copy(q_ref.at[:, last_columns], q_last))
    head_own.append(local_copy(dest_ref, dests.at[local]))

    piece_own.wait()
    for k in range(1, 8):
        source = (member - k + 8) % 8
        copies.arrive(piece_sems[k - 1], w_pieces.at[source], in_octet(source))
    row = lax.broadcasted_iota(jnp.int32, (ROWS, 512), 0)
    column = lax.broadcasted_iota(jnp.int32, (ROWS, 512), 1)
    inner = column % 64
    choose = one_hot((row == (column // 64) * 50 + inner) & (inner < 50))
    tile = dot(choose, w_pieces[...].reshape(512, COLS)).astype(BF)
    weight[me["y"], me["z"] // 4, me["z"] % 4, me["x"]] = tile
    gathers = [ring(copies, weight, me, part) for part in PARTS]

    def advance():
        for gather in gathers:
            next(gather, None)

    advance()

    grad_sems = [copies.new() for _ in range(2)]
    for half in range(2):
        there = pl.ds(pl.multiple_of((2 * half + 1 - core) * 2048, 2048), 2048)
        here = pl.ds(pl.multiple_of((2 * half + core) * 2048, 2048), 2048)
        into = pl.ds(half * 2048, 2048)
        copies.start(
            grad_sems[half],
            grad_ref.at[0, :, there],
            grads.at[core, :, into],
            sibling,
        )
        local_copy(grad_ref.at[0, :, here], grads.at[core, :, into])
    grad_own = locals_[-2:]

    for _ in range(3):
        advance()

    for copy in head_own:
        copy.wait()
    for k in range(1, 8):
        source = (local - k + 8) % 8
        for i in range(3):
            copies.arrive(head_sems[k - 1][i], qkv.at[source, i], in_block(source))
        for i in range(2):
            copies.arrive(
                head_sems[k - 1][3 + i], kv_last.at[source, i], in_block(source)
            )
        copies.arrive(head_sems[k - 1][5], dests.at[source], in_block(source))
    block = mp // 2
    ends = []
    total = 0
    for i in range(3):
        total = total + lengths[i, block]
        ends.append(total)
    key_segments = segments((1, BLOCK), 1, 0, ends)

    def attend_chunk(i, carry):
        columns = pl.ds(pl.multiple_of((i // 4) * HD, HD), HD)
        tiles = pl.ds((i % 4) * 2, 2)
        q = qkv[tiles, 0, :, columns].reshape(2 * TILE, HD)
        k = qkv[:, 1, :, columns].reshape(BLOCK, HD)
        v = qkv[:, 2, :, columns].reshape(BLOCK, HD)
        same = segments((2 * TILE, 1), 0, (i % 4) * 2 * TILE, ends) == key_segments
        mixed[tiles, :, columns] = attend(q, k, v, same).reshape(2, TILE, HD)
        return carry

    def advance_z():
        for gather in gathers[:2]:
            next(gather, None)

    advance_z()
    for head in range(3):
        lax.fori_loop(4 * head, 4 * head + 4, attend_chunk, 0)
    advance_z()
    same = segments((TILE, 1), 0, local * TILE, ends) == key_segments
    last = attend(
        q_last[...],
        kv_last[:, 0].reshape(BLOCK, HD),
        kv_last[:, 1].reshape(BLOCK, HD),
        same,
    )
    own_placing = placing(dests[local])
    staged_last[...] = (
        dot(own_placing.astype(BF), last).astype(BF).reshape(4, CAP, HD)
    )
    last_sems = [copies.new() for _ in range(3)]
    for k in range(1, 4):
        to = (section + k) % 4
        copies.start(
            last_sems[k - 1],
            staged_last.at[to],
            slots.at[to % 2, section, :, last_columns],
            in_section(to),
        )
    last_own = local_copy(
        staged_last.at[section], slots.at[core, section, :, last_columns]
    )

    def place_tile(tile, carry):
        placed = dot(placing(dests[tile]).astype(BF), mixed[tile]).astype(BF)
        staged[tile // 4, :, tile % 4] = placed.reshape(4, CAP, OWN)
        return carry

    lax.fori_loop(0, 8, place_tile, 0)
    slot_sems = [copies.new() for _ in range(7)]
    own_columns = pl.ds(pl.multiple_of(local * OWN, HD), OWN)
    for k in range(1, 8):
        to = (local + k) % 8
        copies.start(
            slot_sems[k - 1],
            staged.at[to // 4, to % 4],
            slots.at[to % 2, :, :, own_columns],
            in_block(to),
        )
    slot_own = local_copy(
        staged.at[local // 4, local % 4], slots.at[core, :, :, own_columns]
    )
    advance()

    relay_sems = [copies.new() for _ in range(9)]

    def relay(index, columns):
        copies.start(
            relay_sems[index],
            slots.at[core, :, :, columns],
            slots.at[core, :, :, columns],
            sibling,
        )

    last_own.wait()
    for k in range(1, 4):
        source = (section - k + 4) % 4
        copies.arrive(
            last_sems[k - 1],
            slots.at[core, source, :, last_columns],
            in_section(source),
        )
    relay(8, last_columns)
    slot_own.wait()
    relay(0, own_columns)
    for k in range(1, 8):
        source = (local - k + 8) % 8
        columns = pl.ds(pl.multiple_of(source * OWN, HD), OWN)
        copies.arrive(
            slot_sems[k - 1], slots.at[core, :, :, columns], in_block(source)
        )
        relay(k, columns)
    advance_z()
    other_local = local + 1 - 2 * core
    for k in range(8):
        source = (other_local - k + 8) % 8
        columns = pl.ds(pl.multiple_of(source * OWN, HD), OWN)
        copies.arrive(relay_sems[k], slots.at[1 - core, :, :, columns], sibling)
    copies.arrive(relay_sems[8], slots.at[1 - core, :, :, last_columns], sibling)

    window_row = lax.broadcasted_iota(jnp.int32, (512, OWN), 0)
    window_column = lax.broadcasted_iota(jnp.int32, (512, OWN), 1)

    def reorder(group, carry):
        window = slots[
            :, :, :, pl.ds(pl.multiple_of(group * OWN, HD), 512)
        ].reshape(512, 512)
        moved = dot(
            window, one_hot(window_row == window_column + 16 * group)
        ).astype(BF)
        for i in range(3):
            lhs[:, pl.ds(pl.multiple_of(i * 1024 + group * HD, HD), HD)] = moved[
                :, i * HD : (i + 1) * HD
            ]
        return carry

    lax.fori_loop(0, 8, reorder, 0)
    lane = lax.broadcasted_iota(jnp.int32, (512, HD), 1) // 16
    tail = jnp.zeros((512, HD), F32)
    for group in range(8):
        piece = slots[:, :, :, OWN * (group + 1) : OWN * (group + 1) + HD]
        tail = jnp.where(lane == group, piece.reshape(512, HD).astype(F32), tail)
    lhs[:, LAST:] = tail.astype(BF)

    for copy in grad_own:
        copy.wait()
    for half in range(2):
        copies.arrive(
            grad_sems[half],
            grads.at[1 - core, :, pl.ds(half * 2048, 2048)],
            sibling,
        )
    back[...] = jnp.zeros_like(back)

    def chunk(i):
        low, x = i // 4, i % 4
        column = (low % 2) * 2048 + ((low // 2) * 4 + x) * COLS
        columns = pl.ds(pl.multiple_of(column, COLS), COLS)
        return low, x, columns

    def weight_rows(first, rows, low, x):
        return weight[:, :, low, x, pl.ds(first, rows), :].reshape(8 * rows, COLS)

    def multiply_back(i, carry):
        low, x, columns = chunk(i)
        grad = grads[:, :, columns].reshape(512, COLS)
        for first, rows, start in K_PARTS:
            back[:, pl.ds(start, 8 * rows)] += dot_nt(
                grad, weight_rows(first, rows, low, x)
            )
        return carry

    def multiply(i, carry):
        low, x, columns = chunk(i)
        total = jnp.zeros((512, COLS), F32)
        for first, rows, start in K_PARTS:
            total = total + dot(
                lhs[:, pl.ds(start, 8 * rows)], weight_rows(first, rows, low, x)
            )
        embeds[:, :, columns] = total.astype(BF).reshape(2, 256, COLS)
        return carry

    for gather in gathers:
        for _ in gather:
            pass
    copies.drain()
    lax.fori_loop(0, 16, multiply_back, 0)

    half_rows = pl.ds(pl.multiple_of((1 - core) * 256, 256), 256)
    slots[0] = back[half_rows, :].astype(BF).reshape(4, CAP, DV)
    back_sem = copies.new()
    copies.start(back_sem, slots.at[0], back_in, sibling)
    return_sems = [copies.new() for _ in range(3)]
    returned_own = []

    def add_back():
        copies.arrive(back_sem, back_in, sibling)
        half_rows = pl.ds(pl.multiple_of(core * 256, 256), 256)
        summed = back[half_rows, :] + back_in[...].reshape(256, DV).astype(F32)
        slots[1] = summed.astype(BF).reshape(4, CAP, DV)
        for k in range(1, 4):
            to = (section + k) % 4
            copies.start(
                return_sems[k - 1],
                slots.at[1, to],
                returned.at[section],
                in_section(to),
            )
        returned_own.append(local_copy(slots.at[1, section], returned.at[section]))

    embed_sems = [copies.new() for _ in range(4)]
    embed_own = []
    for low in range(4):
        lax.fori_loop(4 * low, 4 * low + 4, multiply, 0)
        if low == 1:
            add_back()
        half, quarter = low % 2, low // 2
        here = pl.ds(half * 2048 + quarter * 1024, 1024)
        there = pl.ds(
            pl.multiple_of((2 * half + core) * 2048 + quarter * 1024, 1024), 1024
        )
        copies.start(
            embed_sems[low],
            embeds.at[1 - core, :, here],
            embeds_ref.at[0, :, there],
            sibling,
        )
        embed_own.append(
            local_copy(embeds.at[core, :, here], embeds_ref.at[0, :, there])
        )
    returned_own[0].wait()
    for k in range(1, 4):
        source = (section - k + 4) % 4
        copies.arrive(return_sems[k - 1], returned.at[source], in_section(source))
    chosen = dot(
        own_placing.T.astype(BF), returned[...].reshape(256, DV)
    ).astype(BF)
    rows = pl.ds(0, TILE)
    back[rows, :] = jnp.zeros((TILE, DV), F32)
    lane = lax.broadcasted_iota(jnp.int32, (TILE, HD), 1) // 16
    tail = chosen[:, LAST:].astype(F32)
    source_lane = lax.broadcasted_iota(jnp.int32, (OWN, 512), 0)
    target_lane = lax.broadcasted_iota(jnp.int32, (OWN, 512), 1)
    for group in range(8):
        piece = jnp.concatenate(
            [chosen[:, i * 1024 + group * HD : i * 1024 + (group + 1) * HD] for i in range(3)],
            axis=1,
        )
        moved = dot(piece, one_hot(target_lane == source_lane + 16 * group))
        back[rows, group * OWN : group * OWN + 512] += moved
        back[rows, (group + 1) * OWN : (group + 1) * OWN + HD] += jnp.where(
            lane == group, tail, 0.0
        )
    vgrad_ref[...] = back[rows, :].astype(BF)

    for copy in embed_own:
        copy.wait()
    for low in range(4):
        half, quarter = low % 2, low // 2
        there = pl.ds(
            pl.multiple_of((2 * half + 1 - core) * 2048 + quarter * 1024, 1024), 1024
        )
        copies.arrive(embed_sems[low], embeds_ref.at[0, :, there], sibling)
    copies.drain()


def on_device(query_rows, key_rows, value_rows, image_lengths, dest_group, proj_weight, llm_grad):
    any_ = pl.BlockSpec(memory_space=pl.ANY)
    in_vmem = pl.BlockSpec(memory_space=pltpu.VMEM)
    vmem = pltpu.VMEM
    return pl.pallas_call(
        kernel,
        out_shape=(
            jax.ShapeDtypeStruct(llm_grad.shape, BF),
            jax.ShapeDtypeStruct(query_rows.shape, BF),
        ),
        in_specs=[pl.BlockSpec(memory_space=pltpu.SMEM), in_vmem, any_, any_, any_, in_vmem, any_],
        out_specs=(any_, pl.BlockSpec(memory_space=pltpu.VMEM)),
        scratch_shapes=[
            vmem((64, 2048), BF),
            vmem((8, TILE), jnp.int32),
            vmem((4, 2, 4, 4, ROWS, COLS), BF),
            vmem((8, 64, COLS), BF),
            vmem((8, 3, TILE, OWN), BF),
            vmem((8, 2, TILE, HD), BF),
            vmem((TILE, HD), BF),
            vmem((8, 8, TILE), jnp.int32),
            vmem((8, TILE, OWN), BF),
            vmem((2, 4, 4, CAP, OWN), BF),
            vmem((4, CAP, HD), BF),
            vmem((2, 4, CAP, DV), BF),
            vmem((512, DV), BF),
            vmem((2, 256, 4096), BF),
            vmem((2, 256, 4096), BF),
            vmem((512, DV), F32),
            vmem((4, CAP, DV), BF),
            vmem((4, CAP, DV), BF),
            pltpu.SemaphoreType.DMA((192,)),
            pltpu.SemaphoreType.DMA((192,)),
            pltpu.SemaphoreType.DMA((32,)),
        ],
        compiler_params=pltpu.CompilerParams(
            collective_id=0, has_side_effects=True, vmem_limit_bytes=64 * 1024 * 1024
        ),
    )(image_lengths.T, dest_group, query_rows, key_rows, value_rows, proj_weight, llm_grad)


def solution(mesh):
    placed = (
        P(("mp", "section"), None),
        P(("mp", "section"), None),
        P(("mp", "section"), None),
        P(),
        P(("mp", "section"), None),
        P("mp", "section"),
        P("section", "mp", None),
    )
    return jax.shard_map(
        on_device,
        mesh=mesh,
        in_specs=placed,
        out_specs=(P("section", "mp", None), P(("mp", "section"), None)),
        check_vma=False,
    )
```
